32 devices in a mesh: sec: 4 (over y, x), tile: 8 (over z, core).
Axes of the slice: x: 2, y: 2, z: 4, core: 2. Of those that a mesh axis runs over, the one named last changes fastest.
Arguments:
- beams: float32 [4, 2, 128, 2048], P('sec', None, 'tile'), may hold values from -6 to 6
- medium: float32 [4, 128, 2048], P('sec', 'tile'), may hold values from -0.3 to 0.3
Outputs:
- exit_fields: float32 [4, 2, 128, 2048], P('sec', None, 'tile')
The draws below stay inside these ranges and needn't reach their ends.
All inputs are finite; a program needn't handle non-finite values.
Results may differ from the reference program's by a relative error of at most 0.00002.
Values sent between devices are 32-bit elements; how exact they have to be, the bound alone decides.
No kernel may reach another device: no remote copies, remote signals or barrier semaphores. Data moves between devices by JAX's collectives and lax.ppermute only.
A program may use at most 64 MiB of HBM per device.

```python
import jax
import jax.numpy as jnp
from jax import lax

COLS = 2048
STEPS = 1
ROWS = 128
SECTIONS = 4
REALIZATIONS = 4


def steps_of(key, shape, pieces, smallest, high):
    def one(dim, shards_of):
        draws = jax.random.uniform(jax.random.fold_in(jax.random.fold_in(key, 6), dim), (shards_of,), jnp.float32, smallest / len(pieces), high / len(pieces))
        return jnp.repeat(jnp.exp(draws), shape[dim] // shards_of).reshape((-1,) + (1,) * (len(shape) - dim - 1))

    level = one(*pieces[0])
    for cut in pieces[1:]:
        level = level * one(*cut)
    return level


def noise(stream_key, shape, deviation, reach, pieces=(), kind=jnp.bfloat16):
    values = jax.random.normal(stream_key, shape, jnp.float32) * deviation
    if len(pieces) > 0:
        values = steps_of(stream_key, shape, pieces, -0.22, 0.18) * values
    return jnp.clip(values, min=-reach, max=reach).astype(kind)


def setup_inputs(seed: int = 0) -> dict:
    streams_of = jax.random.split(jax.random.key(seed), 3)
    return {
        "beams": noise(streams_of[0], (REALIZATIONS, 2, ROWS, COLS), 1.0, 6.0, ((0, 4), (2, 8)), jnp.float32),
        "medium": jnp.clip(jax.random.uniform(streams_of[1], (SECTIONS, ROWS, COLS), jnp.float32, -0.3, 0.3) * steps_of(streams_of[1], (SECTIONS, ROWS, COLS), ((0, 4), (1, 8)), -0.4, 0.0), -0.3, 0.3),
    }


diffract_coef = 0.5
step_length = 0.65


def laplace(envelope):
    pads = [(0, 0)] * (envelope.ndim - 2) + [(1, 1), (1, 1)]
    padded = jnp.pad(envelope, pads)
    return padded[..., :-2, 1:-1] + padded[..., 2:, 1:-1] + padded[..., 1:-1, :-2] + padded[..., 1:-1, 2:] - 4.0 * envelope


def derivative(envelope, medium_ext, inside):
    masked = envelope * inside
    forcing = diffract_coef * laplace(masked) + medium_ext * masked
    return jnp.stack([-forcing[..., 1, :, :], forcing[..., 0, :, :]], axis=-3)


def advance(envelope, medium_ext, inside):
    half_length = 0.5 * step_length
    slope_one = derivative(envelope, medium_ext, inside)
    slope_two = derivative(envelope + half_length * slope_one, medium_ext, inside)
    slope_three = derivative(envelope + half_length * slope_two, medium_ext, inside)
    slope_four = derivative(envelope + step_length * slope_three, medium_ext, inside)
    return envelope + (step_length / 6.0) * (slope_one + 2.0 * slope_two + 2.0 * slope_three + slope_four)


def reference(beams, medium):
    def per_beam(envelope):
        def section(state_field, slab_piece):
            for repeat in range(STEPS):
                state_field = advance(state_field, slab_piece, 1.0)
            return state_field, None

        final_field, unused = lax.scan(section, envelope, medium)
        return final_field

    return lax.map(per_beam, beams)
```

```python
import functools

import jax
import jax.numpy as jnp
from jax import lax
from jax.experimental import pallas as pl
from jax.experimental.pallas import tpu as pltpu
from jax.sharding import PartitionSpec as P

AXES = ("sec", "tile")
LANES = 128
SUBLANES = 8
STAGES = 4

diffract_coef = 0.5
step_length = 0.65


def sec_swap(sec, tiles, k):
    return [(s * tiles + t, (s ^ k) * tiles + t) for s in range(sec) for t in range(tiles)]


def pair_swap(sec, tiles):
    return [(s * tiles + t, s * tiles + (t ^ 1)) for s in range(sec) for t in range(tiles)]


def rim_swap(sec, tiles):
    out = []
    for s in range(sec):
        for t in range(tiles):
            if 0 < t < tiles - 1:
                out.append((s * tiles + t, s * tiles + ((t + 1) ^ 1) - 1))
            else:
                out.append((s * tiles + t, (s ^ 1) * tiles + t))
    return out


def field_kernel(place_ref, *refs, sections, first, rows, cols, steps):
    own_b, pair_b, rim_b = refs[:3]
    own_m = refs[3 : 3 + sections]
    pair_m = refs[3 + sections : 3 + 2 * sections]
    rim_m = refs[3 + 2 * sections : 3 + 3 * sections]
    out_ref = refs[3 + 3 * sections]
    field_a, field_b, work_a, work_b, med, coef = refs[4 + 3 * sections :]
    sec, odd, edge = place_ref[0], place_ref[1], place_ref[2]
    chunks = cols // LANES
    pad = SUBLANES
    depth = STAGES * steps
    mid = pad + rows
    pair_at = pl.multiple_of(jnp.where(odd == 1, pad, mid + rows), SUBLANES)
    rim_at = pl.multiple_of(jnp.where(odd == 1, mid + rows, pad), SUBLANES)
    is_edge = edge == 1

    high = 2 * mid + rows
    row = lax.broadcasted_iota(jnp.int32, (high, LANES), 0)
    outside = is_edge & (row >= rim_at) & (row < rim_at + rows)
    for stage in range(STAGES):
        scale = diffract_coef * step_length / (STAGES - stage)
        coef[stage] = jnp.where(outside, 0.0, scale)

    def load(j, carry):
        col = pl.ds(pl.multiple_of(j * LANES, LANES), LANES)
        for t in range(0, rows, SUBLANES):
            src = pl.ds(t, SUBLANES)
            for part in range(2):
                field_a[j, part, pl.ds(mid + t, SUBLANES), :] = own_b[part, src, col]
                field_a[j, part, pl.ds(pair_at + t, SUBLANES), :] = pair_b[part, src, col]
                field_a[j, part, pl.ds(rim_at + t, SUBLANES), :] = jnp.where(
                    is_edge, 0.0, rim_b[part, src, col]
                )
            for k in range(sections):
                slot = sec ^ k
                for at, piece in ((mid, own_m), (pair_at, pair_m), (rim_at, rim_m)):
                    value = piece[k][0, src, col] * (1.0 / diffract_coef) - 4.0
                    med[slot, j, pl.ds(at + t, SUBLANES), :] = value
        return carry

    lax.fori_loop(0, chunks, load, 0)

    lane = lax.broadcasted_iota(jnp.int32, (SUBLANES, LANES), 1)
    low_lane, high_lane = lane == 0, lane == LANES - 1
    begin, end = field_a, field_b
    level = 0
    for step in range(steps):
        source = begin
        for stage in range(STAGES):
            level += 1
            reach = depth - level
            start = mid - reach
            blocks = -(-(rows + 2 * reach) // SUBLANES)
            target = (work_a, work_b, work_a, end)[stage]
            last = level == depth
            for j in range(chunks):
                for block in range(blocks):
                    at = start + SUBLANES * block
                    here = pl.ds(at, SUBLANES)
                    m = med[first + step, j, here, :]
                    g = coef[stage, here, :]
                    drive = []
                    for part in range(2):
                        w = source[j, part, here, :]
                        rows_sum = (
                            source[j, part, pl.ds(at - 1, SUBLANES), :]
                            + source[j, part, pl.ds(at + 1, SUBLANES), :]
                        )
                        before = source[j - 1, part, here, :] if j > 0 else jnp.zeros_like(w)
                        after = source[j + 1, part, here, :] if j + 1 < chunks else jnp.zeros_like(w)
                        left = pltpu.roll(jnp.where(high_lane, before, w), 1, 1)
                        right = pltpu.roll(jnp.where(low_lane, after, w), LANES - 1, 1)
                        drive.append(g * (rows_sum + (left + right) + m * w))
                    re = begin[j, 0, here, :] - drive[1]
                    im = begin[j, 1, here, :] + drive[0]
                    if last:
                        spot = (pl.ds(SUBLANES * block, SUBLANES), pl.ds(j * LANES, LANES))
                        out_ref[0, spot[0], spot[1]] = re
                        out_ref[1, spot[0], spot[1]] = im
                    else:
                        target[j, 0, here, :] = re
                        target[j, 1, here, :] = im
            source = target
        begin, end = end, begin


def per_device(beams, medium):
    sections, tiles = lax.axis_size("sec"), lax.axis_size("tile")
    _, rows, cols = medium.shape
    sec, tile = lax.axis_index("sec"), lax.axis_index("tile")
    place = jnp.stack(
        [sec, tile % 2, ((tile == 0) | (tile == tiles - 1)).astype(jnp.int32)]
    ).astype(jnp.int32)
    swap = lambda value, pairs: lax.ppermute(value, AXES, pairs)
    pair, rim = pair_swap(sections, tiles), rim_swap(sections, tiles)

    own = [medium] + [
        swap(medium, sec_swap(sections, tiles, k)) for k in range(1, sections)
    ]
    pair_field, rim_field = swap(beams, pair), swap(beams, rim)
    own[1:] = lax.optimization_barrier(tuple(own[1:]) + (rim_field,))[:-1]
    pair_pieces = [swap(piece, pair) for piece in own]
    rim_pieces = [swap(piece, rim) for piece in own]

    chunks = cols // LANES
    high = 2 * SUBLANES + 3 * rows
    field = beams
    group = rows // STAGES
    for first in range(0, sections, group):
        steps = min(group, sections - first)
        if first > 0:
            pair_field, rim_field = swap(field, pair), swap(field, rim)
        whole = pl.BlockSpec(memory_space=pltpu.VMEM)
        field = pl.pallas_call(
            functools.partial(
                field_kernel, sections=sections, first=first, rows=rows, cols=cols, steps=steps
            ),
            out_shape=jax.ShapeDtypeStruct((2, rows, cols), jnp.float32),
            in_specs=[pl.BlockSpec(memory_space=pltpu.SMEM)] + [whole] * (3 + 3 * sections),
            out_specs=whole,
            scratch_shapes=[pltpu.VMEM((chunks, 2, high, LANES), jnp.float32)] * 4
            + [
                pltpu.VMEM((sections, chunks, high, LANES), jnp.float32),
                pltpu.VMEM((STAGES, high, LANES), jnp.float32),
            ],
            compiler_params=pltpu.CompilerParams(vmem_limit_bytes=48 * 2**20),
            name="sections_of_field",
        )(place, field.reshape(2, rows, cols), pair_field.reshape(2, rows, cols),
          rim_field.reshape(2, rows, cols), *own, *pair_pieces, *rim_pieces)[None]
    return field


def solution(mesh):
    placed = (P("sec", None, "tile", None), P("sec", "tile", None))
    return jax.shard_map(
        per_device,
        mesh=mesh,
        in_specs=placed,
        out_specs=P("sec", None, "tile", None),
        check_vma=False,
    )
```

```python
import functools

import jax
import jax.numpy as jnp
from jax import lax
from jax.experimental import pallas as pl
from jax.experimental.pallas import tpu as pltpu
from jax.sharding import PartitionSpec as P

AXES = ("sec", "tile")
LANES = 128
SUBLANES = 8
STAGES = 4

diffract_coef = 0.5
step_length = 0.65


def sec_swap(sec, tiles, k):
    return [(s * tiles + t, (s ^ k) * tiles + t) for s in range(sec) for t in range(tiles)]


def pair_swap(sec, tiles):
    return [(s * tiles + t, s * tiles + (t ^ 1)) for s in range(sec) for t in range(tiles)]


def rim_swap(sec, tiles):
    out = []
    for s in range(sec):
        for t in range(tiles):
            if 0 < t < tiles - 1:
                out.append((s * tiles + t, s * tiles + ((t + 1) ^ 1) - 1))
            else:
                out.append((s * tiles + t, (s ^ 1) * tiles + t))
    return out


def stage_scale(stage):
    return diffract_coef * step_length / (STAGES - stage)


def run_stage(source, begin, med, start, blocks, chunks, scale_of, store):
    lane = lax.broadcasted_iota(jnp.int32, (SUBLANES, LANES), 1)
    low_lane, high_lane = lane == 0, lane == LANES - 1
    for j in range(chunks):
        for block in range(blocks):
            at = start + SUBLANES * block
            here = pl.ds(at, SUBLANES)
            m = med[j, here, :]
            g = scale_of(here)
            drive = []
            for part in range(2):
                w = source[j, part, here, :]
                rows_sum = (
                    source[j, part, pl.ds(at - 1, SUBLANES), :]
                    + source[j, part, pl.ds(at + 1, SUBLANES), :]
                )
                before = source[j - 1, part, here, :] if j > 0 else jnp.zeros_like(w)
                after = source[j + 1, part, here, :] if j + 1 < chunks else jnp.zeros_like(w)
                left = pltpu.roll(jnp.where(high_lane, before, w), 1, 1)
                right = pltpu.roll(jnp.where(low_lane, after, w), LANES - 1, 1)
                drive.append(g * (rows_sum + (left + right) + m * w))
            store(j, block, 0, here, begin[j, 0, here, :] - drive[1])
            store(j, block, 1, here, begin[j, 1, here, :] + drive[0])


def row_groups(rows):
    return range(0, rows, SUBLANES)


def columns(j):
    return pl.ds(pl.multiple_of(j * LANES, LANES), LANES)


def to_medium_term(value):
    return value * (1.0 / diffract_coef) - 4.0


def inner_kernel(place_ref, *refs, sections, first, rows, cols, steps):
    own_b, pair_b, rim_b = refs[:3]
    own_m = refs[3 : 3 + sections]
    pair_m = refs[3 + sections]
    edge_ref = refs[4 + sections]
    field_a, field_b, work_a, work_b, med = refs[5 + sections :]
    sec, odd, edge = place_ref[0], place_ref[1], place_ref[2]
    chunks = cols // LANES
    depth = STAGES * steps
    mid = SUBLANES + rows
    pair_at = pl.multiple_of(jnp.where(odd == 1, SUBLANES, mid + rows), SUBLANES)
    rim_at = pl.multiple_of(jnp.where(odd == 1, mid + rows, SUBLANES), SUBLANES)
    is_edge = edge == 1

    def load(j, carry):
        col = columns(j)
        for t in row_groups(rows):
            src = pl.ds(t, SUBLANES)
            for part in range(2):
                field_a[j, part, pl.ds(mid + t, SUBLANES), :] = own_b[part, src, col]
                field_a[j, part, pl.ds(pair_at + t, SUBLANES), :] = pair_b[part, src, col]
                field_a[j, part, pl.ds(rim_at + t, SUBLANES), :] = jnp.where(
                    is_edge, 0.0, rim_b[part, src, col]
                )
            for k in range(sections):
                slot = sec ^ k
                med[slot, j, pl.ds(mid + t, SUBLANES), :] = to_medium_term(own_m[k][0, src, col])
                med[slot, j, pl.ds(pair_at + t, SUBLANES), :] = to_medium_term(
                    pair_m[k, src, col]
                )
        return carry

    lax.fori_loop(0, chunks, load, 0)

    low = pl.multiple_of(jnp.where(odd == 1, SUBLANES, mid), SUBLANES)
    begin, end = field_a, field_b
    level = 0
    for step in range(steps):
        source = begin
        for stage in range(STAGES):
            level += 1
            if level == depth:
                break
            target = (work_a, work_b, work_a, end)[stage]

            def store(j, block, part, here, value, target=target):
                target[j, part, here, :] = value

            run_stage(
                source, begin, med.at[first + step], low + level,
                -(-(2 * (rows - level)) // SUBLANES), chunks,
                lambda here, stage=stage: stage_scale(stage), store,
            )
            edge_at = jnp.where(odd == 1, mid + rows - SUBLANES - level, mid + level)
            for j in range(chunks):
                for part in range(2):
                    edge_ref[level - 1, j, part, :, :] = target[
                        j, part, pl.ds(edge_at, SUBLANES), :
                    ]
            source = target
        begin, end = end, begin


def outer_kernel(place_ref, *refs, sections, first, rows, cols, steps):
    own_b, rim_b = refs[:2]
    own_m = refs[2 : 2 + sections]
    rim_m, edge_ref, out_ref = refs[2 + sections : 5 + sections]
    field_a, field_b, work_a, work_b, med, coef = refs[5 + sections :]
    sec, odd, edge = place_ref[0], place_ref[1], place_ref[2]
    chunks = cols // LANES
    depth = STAGES * steps
    mid = SUBLANES + rows
    rim_at = pl.multiple_of(jnp.where(odd == 1, mid + rows, SUBLANES), SUBLANES)
    is_edge = edge == 1

    high = 2 * mid + rows
    row = lax.broadcasted_iota(jnp.int32, (high, LANES), 0)
    outside = is_edge & (row >= rim_at) & (row < rim_at + rows)
    for stage in range(STAGES):
        coef[stage] = jnp.where(outside, 0.0, stage_scale(stage))

    def load(j, carry):
        col = columns(j)
        for t in row_groups(rows):
            src = pl.ds(t, SUBLANES)
            for part in range(2):
                field_a[j, part, pl.ds(mid + t, SUBLANES), :] = own_b[part, src, col]
                field_a[j, part, pl.ds(rim_at + t, SUBLANES), :] = jnp.where(
                    is_edge, 0.0, rim_b[part, src, col]
                )
            for k in range(sections):
                med[sec ^ k, j, pl.ds(mid + t, SUBLANES), :] = to_medium_term(
                    own_m[k][0, src, col]
                )
        at = 0
        for step, count in enumerate(rim_rows(rows, steps)):
            skip = jnp.where(odd == 1, 0, rows - count)
            for t in row_groups(count):
                to = pl.multiple_of(rim_at + skip + t, SUBLANES)
                med[first + step, j, pl.ds(to, SUBLANES), :] = to_medium_term(
                    rim_m[pl.ds(at + t, SUBLANES), col]
                )
            at += count
        return carry

    lax.fori_loop(0, chunks, load, 0)

    begin, end = field_a, field_b
    level = 0
    for step in range(steps):
        source = begin
        for stage in range(STAGES):
            if level > 0:
                edge_at = jnp.where(odd == 1, mid + rows - SUBLANES - level, mid + level)
                for j in range(chunks):
                    for part in range(2):
                        source[j, part, pl.ds(edge_at, SUBLANES), :] = edge_ref[
                            level - 1, j, part, :, :
                        ]
            level += 1
            target = (work_a, work_b, work_a, end)[stage]
            if level < depth:

                def store(j, block, part, here, value, target=target):
                    target[j, part, here, :] = value

            else:

                def store(j, block, part, here, value):
                    out_ref[part, pl.ds(SUBLANES * block, SUBLANES), columns(j)] = value

            run_stage(
                source, begin, med.at[first + step],
                jnp.where(odd == 1, mid + depth - level, mid + level - depth),
                rows // SUBLANES, chunks,
                lambda here, stage=stage: coef[stage, here, :], store,
            )
            source = target
        begin, end = end, begin


def rim_rows(rows, steps):
    return [
        -(-(STAGES * (steps - step) - 1) // SUBLANES) * SUBLANES for step in range(steps)
    ]


def pack_rim(own, sec, odd, rows, first, steps):
    parts = []
    for step, count in enumerate(rim_rows(rows, steps)):
        cut = lambda piece: (
            piece[0] if count == rows
            else jnp.where(odd == 1, piece[0, rows - count :], piece[0, :count])
        )
        part = cut(own[0])
        for k in range(1, len(own)):
            part = jnp.where((sec ^ k) == first + step, cut(own[k]), part)
        parts.append(part)
    return jnp.concatenate(parts, axis=0)


def per_device(beams, medium):
    sections, tiles = lax.axis_size("sec"), lax.axis_size("tile")
    _, rows, cols = medium.shape
    sec, tile = lax.axis_index("sec"), lax.axis_index("tile")
    odd = tile % 2
    place = jnp.stack(
        [sec, odd, ((tile == 0) | (tile == tiles - 1)).astype(jnp.int32)]
    ).astype(jnp.int32)
    swap = lambda value, pairs: lax.ppermute(value, AXES, pairs)
    pair, rim = pair_swap(sections, tiles), rim_swap(sections, tiles)

    own = [medium] + [
        swap(medium, sec_swap(sections, tiles, k)) for k in range(1, sections)
    ]
    pair_pieces = swap(jnp.concatenate(own, axis=0), pair)

    chunks = cols // LANES
    high = 2 * SUBLANES + 3 * rows
    smem = pl.BlockSpec(memory_space=pltpu.SMEM)
    whole = pl.BlockSpec(memory_space=pltpu.VMEM)
    buffers = [pltpu.VMEM((chunks, 2, high, LANES), jnp.float32)] * 4 + [
        pltpu.VMEM((sections, chunks, high, LANES), jnp.float32)
    ]
    params = pltpu.CompilerParams(vmem_limit_bytes=40 * 2**20)
    field = beams
    group = rows // STAGES
    for first in range(0, sections, group):
        steps = min(group, sections - first)
        depth = STAGES * steps
        pair_field, rim_field = swap(field, pair), swap(field, rim)
        *own, rim_field = lax.optimization_barrier((*own, rim_field))
        rim_pack = swap(pack_rim(own, sec, odd, rows, first, steps), rim)
        fixed = dict(sections=sections, first=first, rows=rows, cols=cols, steps=steps)
        own_field, pair_field, rim_field = (
            value.reshape(2, rows, cols) for value in (field, pair_field, rim_field)
        )
        work = 36 * 2 * SUBLANES * cols
        edges = pl.pallas_call(
            functools.partial(inner_kernel, **fixed),
            out_shape=jax.ShapeDtypeStruct(
                (depth - 1, chunks, 2, SUBLANES, LANES), jnp.float32
            ),
            in_specs=[smem] + [whole] * (4 + sections),
            out_specs=whole,
            scratch_shapes=buffers,
            compiler_params=params,
            cost_estimate=pl.CostEstimate(
                flops=10 * work, bytes_accessed=16 * work, transcendentals=0
            ),
            name="inner_rows",
        )(place, own_field, pair_field, rim_field, *own, pair_pieces)
        field = pl.pallas_call(
            functools.partial(outer_kernel, **fixed),
            out_shape=jax.ShapeDtypeStruct((2, rows, cols), jnp.float32),
            in_specs=[smem] + [whole] * (4 + sections),
            out_specs=whole,
            scratch_shapes=buffers + [pltpu.VMEM((STAGES, high, LANES), jnp.float32)],
            compiler_params=params,
            name="outer_rows",
        )(place, own_field, rim_field, *own, rim_pack, edges)[None]
    return field


def solution(mesh):
    placed = (P("sec", None, "tile", None), P("sec", "tile", None))
    return jax.shard_map(
        per_device,
        mesh=mesh,
        in_specs=placed,
        out_specs=P("sec", None, "tile", None),
        check_vma=False,
    )
```

```python
import functools

import jax
import jax.numpy as jnp
from jax import lax
from jax.experimental import pallas as pl
from jax.experimental.pallas import tpu as pltpu
from jax.sharding import PartitionSpec as P

AXES = ("sec", "tile")
LANES = 128
SUBLANES = 8
STAGES = 4
OUT_PARTS = 4

diffract_coef = 0.5
step_length = 0.65


def sec_swap(sec, tiles, k):
    return [(s * tiles + t, (s ^ k) * tiles + t) for s in range(sec) for t in range(tiles)]


def pair_swap(sec, tiles):
    return [(s * tiles + t, s * tiles + (t ^ 1)) for s in range(sec) for t in range(tiles)]


def rim_swap(sec, tiles):
    out = []
    for s in range(sec):
        for t in range(tiles):
            if 0 < t < tiles - 1:
                out.append((s * tiles + t, s * tiles + ((t + 1) ^ 1) - 1))
            else:
                out.append((s * tiles + t, (s ^ 1) * tiles + t))
    return out


def stage_scale(stage):
    return diffract_coef * step_length / (STAGES - stage)


def run_stage(source, begin, med, start, blocks, chunks, scale_of, store):
    lane = lax.broadcasted_iota(jnp.int32, (SUBLANES, LANES), 1)
    low_lane, high_lane = lane == 0, lane == LANES - 1
    for j in range(chunks):
        for block in range(blocks):
            at = start + SUBLANES * block
            here = pl.ds(at, SUBLANES)
            m = med[j, here, :]
            g = scale_of(here)
            drive = []
            for part in range(2):
                w = source[j, part, here, :]
                rows_sum = (
                    source[j, part, pl.ds(at - 1, SUBLANES), :]
                    + source[j, part, pl.ds(at + 1, SUBLANES), :]
                )
                before = source[j - 1, part, here, :] if j > 0 else jnp.zeros_like(w)
                after = source[j + 1, part, here, :] if j + 1 < chunks else jnp.zeros_like(w)
                left = pltpu.roll(jnp.where(high_lane, before, w), 1, 1)
                right = pltpu.roll(jnp.where(low_lane, after, w), LANES - 1, 1)
                drive.append(g * (rows_sum + (left + right) + m * w))
            store(j, block, 0, here, begin[j, 0, here, :] - drive[1])
            store(j, block, 1, here, begin[j, 1, here, :] + drive[0])


def row_groups(rows):
    return range(0, rows, SUBLANES)


def columns(j):
    return pl.ds(j * LANES, LANES)


def to_medium_term(value):
    return value * (1.0 / diffract_coef) - 4.0


def by_side(odd, body):
    pl.when(odd == 1)(functools.partial(body, True))
    pl.when(odd == 0)(functools.partial(body, False))


def inner_kernel(place_ref, *refs, sections, first, rows, cols, steps):
    own_b, pair_b = refs[:2]
    own_m = refs[2 : 2 + sections]
    pair_m = refs[2 + sections]
    edge_ref = refs[3 + sections]
    field_a, field_b, work_a, work_b, med = refs[4 + sections :]
    sec, odd = place_ref[0], place_ref[1]
    chunks = cols // LANES
    depth = STAGES * steps
    mid = SUBLANES + rows

    def run(is_odd):
        low = SUBLANES if is_odd else mid
        pair_at = SUBLANES if is_odd else mid + rows
        for j in range(chunks):
            col = columns(j)
            for t in row_groups(rows):
                src = pl.ds(t, SUBLANES)
                for part in range(2):
                    field_a[j, part, pl.ds(mid + t, SUBLANES), :] = own_b[part, src, col]
                    field_a[j, part, pl.ds(pair_at + t, SUBLANES), :] = pair_b[part, src, col]
                for k in range(sections):
                    slot = sec ^ k
                    med[slot, j, pl.ds(mid + t, SUBLANES), :] = to_medium_term(
                        own_m[k][0, src, col]
                    )
                    med[slot, j, pl.ds(pair_at + t, SUBLANES), :] = to_medium_term(
                        pair_m[k, src, col]
                    )
        begin, end = field_a, field_b
        level = 0
        for step in range(steps):
            source = begin
            for stage in range(STAGES):
                level += 1
                if level == depth:
                    break
                target = (work_a, work_b, work_a, end)[stage]

                def store(j, block, part, here, value, target=target):
                    target[j, part, here, :] = value

                run_stage(
                    source, begin, med.at[first + step], low + level,
                    -(-(2 * (rows - level)) // SUBLANES), chunks,
                    lambda here, stage=stage: stage_scale(stage), store,
                )
                edge_at = mid + rows - SUBLANES - level if is_odd else mid + level
                for j in range(chunks):
                    for part in range(2):
                        edge_ref[level - 1, j, part, :, :] = target[
                            j, part, pl.ds(edge_at, SUBLANES), :
                        ]
                source = target
            begin, end = end, begin

    by_side(odd, run)


def outer_kernel(place_ref, *refs, sections, first, rows, cols, steps):
    own_b, rim_b = refs[:2]
    own_m = refs[2 : 2 + sections]
    rim_m, edge_ref, out_ref, levels, med, coef, result, sems = refs[2 + sections :]
    sec, odd, edge = place_ref[0], place_ref[1], place_ref[2]
    chunks = cols // LANES
    depth = STAGES * steps
    mid = SUBLANES + rows
    is_edge = edge == 1
    parts = sems.shape[0]
    per_part = chunks // parts

    def run(is_odd):
        rim_at = mid + rows if is_odd else SUBLANES
        row = lax.broadcasted_iota(jnp.int32, coef.shape[1:], 0)
        outside = is_edge & (row >= rim_at) & (row < rim_at + rows)
        for stage in range(STAGES):
            coef[stage] = jnp.where(outside, 0.0, stage_scale(stage))
        for j in range(chunks):
            col = columns(j)
            for t in row_groups(rows):
                src = pl.ds(t, SUBLANES)
                for part in range(2):
                    levels[0, j, part, pl.ds(rim_at + t, SUBLANES), :] = jnp.where(
                        is_edge, 0.0, rim_b[part, src, col]
                    )
            near = rows - SUBLANES if is_odd else 0
            for part in range(2):
                levels[0, j, part, pl.ds(mid + near, SUBLANES), :] = own_b[
                    part, pl.ds(near, SUBLANES), col
                ]
            for k in range(sections):
                for t in row_groups(rows):
                    med[sec ^ k, j, pl.ds(mid + t, SUBLANES), :] = to_medium_term(
                        own_m[k][0, pl.ds(t, SUBLANES), col]
                    )
            at = 0
            for step, count in enumerate(rim_rows(rows, steps)):
                over = -count % SUBLANES
                there = mid + rows if is_odd else mid - count - over
                for t in row_groups(count):
                    here = at + t - (0 if is_odd else over)
                    if is_odd and here + SUBLANES > rim_m.shape[1]:
                        size = rim_m.shape[1] - here
                    else:
                        size = SUBLANES
                    med[first + step, j, pl.ds(there + t, size), :] = to_medium_term(
                        rim_m[j, pl.ds(here, size), :]
                    )
                at += count
            for level in range(1, depth):
                edge_at = mid + rows - SUBLANES - level if is_odd else mid + level
                for part in range(2):
                    levels[level, j, part, pl.ds(edge_at, SUBLANES), :] = edge_ref[
                        level - 1, j, part, :, :
                    ]

        copies = [
            pltpu.make_async_copy(
                result.at[:, :, pl.ds(p * per_part * LANES, per_part * LANES)],
                out_ref.at[:, :, pl.ds(p * per_part * LANES, per_part * LANES)],
                sems.at[p],
            )
            for p in range(parts)
        ]
        level = 0
        for step in range(steps):
            begin = levels.at[level]
            for stage in range(STAGES):
                level += 1

                def store(j, block, part, here, value, level=level):
                    if level < depth:
                        levels[level, j, part, here, :] = value
                        return
                    result[part, pl.ds(SUBLANES * block, SUBLANES), columns(j)] = value
                    if part == 1 and block + 1 == rows // SUBLANES and (j + 1) % per_part == 0:
                        copies[j // per_part].start()

                run_stage(
                    levels.at[level - 1], begin, med.at[first + step],
                    mid + depth - level if is_odd else mid + level - depth,
                    rows // SUBLANES, chunks,
                    lambda here, stage=stage: coef[stage, here, :], store,
                )
        for copy in copies:
            copy.wait()

    by_side(odd, run)


def rim_rows(rows, steps):
    return [STAGES * (steps - step) for step in range(steps)]


def pack_kernel(place_ref, *refs, sections, first, rows, cols, steps):
    own_m, rim_out = refs[:sections], refs[sections]
    sec, odd = place_ref[0], place_ref[1]
    chunks = cols // LANES

    def pack(k, at, lo, hi):
        def body():
            for t in row_groups(rows):
                cut_lo, cut_hi = max(lo, t), min(hi, t + SUBLANES)
                if cut_lo < cut_hi:
                    for j in range(chunks):
                        rim_out[j, pl.ds(at + cut_lo - lo, cut_hi - cut_lo), :] = own_m[k][
                            0, pl.ds(cut_lo, cut_hi - cut_lo), columns(j)
                        ]

        return body

    at = 0
    for step, count in enumerate(rim_rows(rows, steps)):
        for k in range(sections):
            mine = (sec ^ k) == first + step
            pl.when(mine & (odd == 1))(pack(k, at, rows - count, rows))
            pl.when(mine & (odd == 0))(pack(k, at, 0, count))
        at += count


def load_kernel(field_ref, medium_ref, field_out, medium_out, field_sem, medium_sem):
    copies = (
        pltpu.make_async_copy(medium_ref, medium_out, medium_sem),
        pltpu.make_async_copy(field_ref, field_out, field_sem),
    )
    for copy in copies:
        copy.start()
    for copy in copies:
        copy.wait()


def per_device(beams, medium):
    sections, tiles = lax.axis_size("sec"), lax.axis_size("tile")
    _, rows, cols = medium.shape
    sec, tile = lax.axis_index("sec"), lax.axis_index("tile")
    odd = tile % 2
    place = jnp.stack(
        [sec, odd, ((tile == 0) | (tile == tiles - 1)).astype(jnp.int32)]
    ).astype(jnp.int32)
    swap = lambda value, pairs: lax.ppermute(value, AXES, pairs)
    pair, rim = pair_swap(sections, tiles), rim_swap(sections, tiles)

    far = [swap(medium, sec_swap(sections, tiles, k)) for k in range(1, sections)]
    chunks = cols // LANES
    high = 2 * SUBLANES + 3 * rows
    smem = pl.BlockSpec(memory_space=pltpu.SMEM)
    whole = pl.BlockSpec(memory_space=pltpu.VMEM)
    buffers = [pltpu.VMEM((chunks, 2, high, LANES), jnp.float32)] * 4 + [
        pltpu.VMEM((sections, chunks, high, LANES), jnp.float32)
    ]
    params = pltpu.CompilerParams(vmem_limit_bytes=40 * 2**20)
    field, medium = pl.pallas_call(
        load_kernel,
        out_shape=(
            pltpu.VMEM(beams.shape, beams.dtype),
            pltpu.VMEM(medium.shape, medium.dtype),
        ),
        in_specs=[pl.BlockSpec(memory_space=pl.ANY)] * 2,
        out_specs=(whole, whole),
        scratch_shapes=[pltpu.SemaphoreType.DMA(())] * 2,
        cost_estimate=pl.CostEstimate(flops=0, bytes_accessed=2**21, transcendentals=0),
        name="load_arguments",
    )(beams, medium)
    own = [medium] + far
    group = rows // STAGES
    for first in range(0, sections, group):
        steps = min(group, sections - first)
        depth = STAGES * steps
        sent = field if first > 0 else beams
        pair_field, rim_field = swap(sent, pair), swap(sent, rim)
        *own, field = lax.optimization_barrier((*own, field))
        fixed = dict(sections=sections, first=first, rows=rows, cols=cols, steps=steps)
        pair_pack = jnp.concatenate(own, axis=0)
        rim_pack = pl.pallas_call(
            functools.partial(pack_kernel, **fixed),
            out_shape=jax.ShapeDtypeStruct(
                (chunks, sum(rim_rows(rows, steps)), LANES), jnp.float32
            ),
            in_specs=[smem] + [whole] * sections,
            out_specs=whole,
            compiler_params=params,
            name="pack_rows",
        )(place, *own)
        rim_pack, pair_pack = swap(rim_pack, rim), swap(pair_pack, pair)
        own_field, pair_field, rim_field = (
            value.reshape(2, rows, cols) for value in (field, pair_field, rim_field)
        )
        work = 36 * 2 * SUBLANES * cols
        edges = pl.pallas_call(
            functools.partial(inner_kernel, **fixed),
            out_shape=jax.ShapeDtypeStruct(
                (depth - 1, chunks, 2, SUBLANES, LANES), jnp.float32
            ),
            in_specs=[smem] + [whole] * (3 + sections),
            out_specs=whole,
            scratch_shapes=buffers,
            compiler_params=params,
            cost_estimate=pl.CostEstimate(
                flops=10 * work, bytes_accessed=16 * work, transcendentals=0
            ),
            name="inner_rows",
        )(place, own_field, pair_field, *own, pair_pack)
        field = pl.pallas_call(
            functools.partial(outer_kernel, **fixed),
            out_shape=jax.ShapeDtypeStruct((2, rows, cols), jnp.float32),
            in_specs=[smem] + [whole] * (4 + sections),
            out_specs=pl.BlockSpec(memory_space=pl.ANY),
            scratch_shapes=[
                pltpu.VMEM((depth, chunks, 2, high, LANES), jnp.float32),
                pltpu.VMEM((sections, chunks, high, LANES), jnp.float32),
                pltpu.VMEM((STAGES, high, LANES), jnp.float32),
                pltpu.VMEM((2, rows, cols), jnp.float32),
                pltpu.SemaphoreType.DMA((OUT_PARTS,)),
            ],
            compiler_params=params,
            name="outer_rows",
        )(place, own_field, rim_field, *own, rim_pack, edges)[None]
    return field


def solution(mesh):
    placed = (P("sec", None, "tile", None), P("sec", "tile", None))
    return jax.shard_map(
        per_device,
        mesh=mesh,
        in_specs=placed,
        out_specs=P("sec", None, "tile", None),
        check_vma=False,
    )
```

```python
import functools

import jax
import jax.numpy as jnp
from jax import lax
from jax.experimental import pallas as pl
from jax.experimental.pallas import tpu as pltpu
from jax.sharding import PartitionSpec as P

AXES = ("sec", "tile")
LANES = 128
SUBLANES = 8
STAGES = 4
OUT_PARTS = 4

diffract_coef = 0.5
step_length = 0.65


def sec_swap(sec, tiles, k):
    return [(s * tiles + t, (s ^ k) * tiles + t) for s in range(sec) for t in range(tiles)]


def far_bits(k):
    return k ^ (k >> 1)


def pair_swap(sec, tiles):
    return [(s * tiles + t, s * tiles + (t ^ 1)) for s in range(sec) for t in range(tiles)]


def rim_swap(sec, tiles):
    out = []
    for s in range(sec):
        for t in range(tiles):
            if 0 < t < tiles - 1:
                out.append((s * tiles + t, s * tiles + ((t + 1) ^ 1) - 1))
            else:
                out.append((s * tiles + t, (s ^ 1) * tiles + t))
    return out


def stage_scale(stage):
    return diffract_coef * step_length / (STAGES - stage)


def run_stage(source, begin, med, start, blocks, chunks, scale_of, store):
    lane = lax.broadcasted_iota(jnp.int32, (SUBLANES, LANES), 1)
    low_lane, high_lane = lane == 0, lane == LANES - 1
    for j in range(chunks):
        for block in range(blocks):
            at = start + SUBLANES * block
            here = pl.ds(at, SUBLANES)
            m = med[j, here, :]
            g = scale_of(here)
            drive = []
            for part in range(2):
                w = source[j, part, here, :]
                rows_sum = (
                    source[j, part, pl.ds(at - 1, SUBLANES), :]
                    + source[j, part, pl.ds(at + 1, SUBLANES), :]
                )
                before = source[j - 1, part, here, :] if j > 0 else jnp.zeros_like(w)
                after = source[j + 1, part, here, :] if j + 1 < chunks else jnp.zeros_like(w)
                left = pltpu.roll(jnp.where(high_lane, before, w), 1, 1)
                right = pltpu.roll(jnp.where(low_lane, after, w), LANES - 1, 1)
                drive.append(g * (rows_sum + (left + right) + m * w))
            store(j, block, 0, here, begin[j, 0, here, :] - drive[1])
            store(j, block, 1, here, begin[j, 1, here, :] + drive[0])


def row_groups(rows):
    return range(0, rows, SUBLANES)


def columns(j):
    return pl.ds(j * LANES, LANES)


def to_medium_term(value):
    return value * (1.0 / diffract_coef) - 4.0


def by_side(odd, body):
    pl.when(odd == 1)(functools.partial(body, True))
    pl.when(odd == 0)(functools.partial(body, False))


def inner_kernel(*refs, sections, first, rows, cols, steps):
    own_b, pair_b = refs[:2]
    own_m = refs[2 : 2 + sections]
    pair_m = refs[2 + sections]
    edge_ref = refs[3 + sections]
    field_a, field_b, work_a, work_b, med = refs[4 + sections :]
    sec, odd = lax.axis_index("sec"), lax.axis_index("tile") % 2
    chunks = cols // LANES
    depth = STAGES * steps
    mid = SUBLANES + rows

    def run(is_odd):
        low = SUBLANES if is_odd else mid
        pair_at = SUBLANES if is_odd else mid + rows
        for j in range(chunks):
            col = columns(j)
            for t in row_groups(rows):
                src = pl.ds(t, SUBLANES)
                for part in range(2):
                    field_a[j, part, pl.ds(mid + t, SUBLANES), :] = own_b[part, src, col]
                    field_a[j, part, pl.ds(pair_at + t, SUBLANES), :] = pair_b[part, src, col]
                for k in range(sections):
                    slot = sec ^ far_bits(k)
                    med[slot, j, pl.ds(mid + t, SUBLANES), :] = to_medium_term(
                        own_m[k][0, src, col]
                    )
                    med[slot, j, pl.ds(pair_at + t, SUBLANES), :] = to_medium_term(
                        pair_m[k, src, col]
                    )
        begin, end = field_a, field_b
        level = 0
        for step in range(steps):
            source = begin
            for stage in range(STAGES):
                level += 1
                if level == depth:
                    break
                target = (work_a, work_b, work_a, end)[stage]

                def store(j, block, part, here, value, target=target):
                    target[j, part, here, :] = value

                run_stage(
                    source, begin, med.at[first + step], low + level,
                    -(-(2 * (rows - level)) // SUBLANES), chunks,
                    lambda here, stage=stage: stage_scale(stage), store,
                )
                edge_at = mid + rows - SUBLANES - level if is_odd else mid + level
                for j in range(chunks):
                    for part in range(2):
                        edge_ref[level - 1, j, part, :, :] = target[
                            j, part, pl.ds(edge_at, SUBLANES), :
                        ]
                source = target
            begin, end = end, begin

    by_side(odd, run)


def outer_kernel(*refs, tiles, sections, first, rows, cols, steps):
    own_b, rim_b = refs[:2]
    own_m = refs[2 : 2 + sections]
    rim_m, edge_ref, out_ref, levels, med, coef, result, sems = refs[2 + sections :]
    sec, tile = lax.axis_index("sec"), lax.axis_index("tile")
    odd = tile % 2
    chunks = cols // LANES
    depth = STAGES * steps
    mid = SUBLANES + rows
    is_edge = (tile == 0) | (tile == tiles - 1)
    parts = sems.shape[0]
    per_part = chunks // parts

    def run(is_odd):
        rim_at = mid + rows if is_odd else SUBLANES
        row = lax.broadcasted_iota(jnp.int32, coef.shape[1:], 0)
        outside = is_edge & (row >= rim_at) & (row < rim_at + rows)
        for stage in range(STAGES):
            coef[stage] = jnp.where(outside, 0.0, stage_scale(stage))
        for j in range(chunks):
            col = columns(j)
            for t in row_groups(rows):
                src = pl.ds(t, SUBLANES)
                for part in range(2):
                    levels[0, j, part, pl.ds(rim_at + t, SUBLANES), :] = jnp.where(
                        is_edge, 0.0, rim_b[part, src, col]
                    )
            near = rows - SUBLANES if is_odd else 0
            for part in range(2):
                levels[0, j, part, pl.ds(mid + near, SUBLANES), :] = own_b[
                    part, pl.ds(near, SUBLANES), col
                ]
            for k in range(sections):
                for t in row_groups(rows):
                    med[sec ^ far_bits(k), j, pl.ds(mid + t, SUBLANES), :] = to_medium_term(
                        own_m[k][0, pl.ds(t, SUBLANES), col]
                    )
            at = 0
            for step, count in enumerate(rim_rows(rows, steps)):
                over = -count % SUBLANES
                there = mid + rows if is_odd else mid - count - over
                for t in row_groups(count):
                    here = at + t - (0 if is_odd else over)
                    if is_odd and here + SUBLANES > rim_m.shape[1]:
                        size = rim_m.shape[1] - here
                    else:
                        size = SUBLANES
                    med[first + step, j, pl.ds(there + t, size), :] = to_medium_term(
                        rim_m[j, pl.ds(here, size), :]
                    )
                at += count
            for level in range(1, depth):
                edge_at = mid + rows - SUBLANES - level if is_odd else mid + level
                for part in range(2):
                    levels[level, j, part, pl.ds(edge_at, SUBLANES), :] = edge_ref[
                        level - 1, j, part, :, :
                    ]

        copies = [
            pltpu.make_async_copy(
                result.at[:, :, pl.ds(p * per_part * LANES, per_part * LANES)],
                out_ref.at[:, :, pl.ds(p * per_part * LANES, per_part * LANES)],
                sems.at[p],
            )
            for p in range(parts)
        ]
        level = 0
        for step in range(steps):
            begin = levels.at[level]
            for stage in range(STAGES):
                level += 1

                def store(j, block, part, here, value, level=level):
                    if level < depth:
                        levels[level, j, part, here, :] = value
                        return
                    result[part, pl.ds(SUBLANES * block, SUBLANES), columns(j)] = value
                    if part == 1 and block + 1 == rows // SUBLANES and (j + 1) % per_part == 0:
                        copies[j // per_part].start()

                run_stage(
                    levels.at[level - 1], begin, med.at[first + step],
                    mid + depth - level if is_odd else mid + level - depth,
                    rows // SUBLANES, chunks,
                    lambda here, stage=stage: coef[stage, here, :], store,
                )
        for copy in copies:
            copy.wait()

    by_side(odd, run)


def rim_rows(rows, steps):
    return [STAGES * (steps - step) for step in range(steps)]


def pack_kernel(*refs, sections, first, rows, cols, steps):
    own_m, rim_out = refs[:sections], refs[sections]
    sec, odd = lax.axis_index("sec"), lax.axis_index("tile") % 2
    chunks = cols // LANES

    def pack(k, at, lo, hi):
        def body():
            for t in row_groups(rows):
                cut_lo, cut_hi = max(lo, t), min(hi, t + SUBLANES)
                if cut_lo < cut_hi:
                    for j in range(chunks):
                        rim_out[j, pl.ds(at + cut_lo - lo, cut_hi - cut_lo), :] = own_m[k][
                            0, pl.ds(cut_lo, cut_hi - cut_lo), columns(j)
                        ]

        return body

    at = 0
    for step, count in enumerate(rim_rows(rows, steps)):
        for k in range(sections):
            mine = (sec ^ far_bits(k)) == first + step
            pl.when(mine & (odd == 1))(pack(k, at, rows - count, rows))
            pl.when(mine & (odd == 0))(pack(k, at, 0, count))
        at += count


def load_kernel(field_ref, medium_ref, field_out, medium_out, field_sem, medium_sem):
    copies = (
        pltpu.make_async_copy(medium_ref, medium_out, medium_sem),
        pltpu.make_async_copy(field_ref, field_out, field_sem),
    )
    for copy in copies:
        copy.start()
    for copy in copies:
        copy.wait()


def per_device(beams, medium):
    sections, tiles = lax.axis_size("sec"), lax.axis_size("tile")
    _, rows, cols = medium.shape
    swap = lambda value, pairs: lax.ppermute(value, AXES, pairs)
    pair, rim = pair_swap(sections, tiles), rim_swap(sections, tiles)

    far = [swap(medium, sec_swap(sections, tiles, far_bits(k))) for k in range(1, sections)]
    chunks = cols // LANES
    high = 2 * SUBLANES + 3 * rows
    whole = pl.BlockSpec(memory_space=pltpu.VMEM)
    buffers = [pltpu.VMEM((chunks, 2, high, LANES), jnp.float32)] * 4 + [
        pltpu.VMEM((sections, chunks, high, LANES), jnp.float32)
    ]
    params = pltpu.CompilerParams(vmem_limit_bytes=40 * 2**20)
    field, medium = pl.pallas_call(
        load_kernel,
        out_shape=(
            pltpu.VMEM(beams.shape, beams.dtype),
            pltpu.VMEM(medium.shape, medium.dtype),
        ),
        in_specs=[pl.BlockSpec(memory_space=pl.ANY)] * 2,
        out_specs=(whole, whole),
        scratch_shapes=[pltpu.SemaphoreType.DMA(())] * 2,
        cost_estimate=pl.CostEstimate(flops=0, bytes_accessed=2**21, transcendentals=0),
        name="load_arguments",
    )(beams, medium)
    own = [medium] + far
    group = rows // STAGES
    for first in range(0, sections, group):
        steps = min(group, sections - first)
        depth = STAGES * steps
        pair_field = swap(field if first > 0 else beams, pair)
        rim_parts = [swap(field[:, part], rim) for part in range(2)]
        *own, field = lax.optimization_barrier((*own, field))
        fixed = dict(sections=sections, first=first, rows=rows, cols=cols, steps=steps)
        rim_pack = pl.pallas_call(
            functools.partial(pack_kernel, **fixed),
            out_shape=jax.ShapeDtypeStruct(
                (chunks, sum(rim_rows(rows, steps)), LANES), jnp.float32
            ),
            in_specs=[whole] * sections,
            out_specs=whole,
            compiler_params=params,
            name="pack_rows",
        )(*own)
        *near, re, im, _ = lax.optimization_barrier((*own, *rim_parts, rim_pack))
        rim_field = jnp.stack([re, im], axis=1)
        rim_pack = swap(rim_pack, rim)
        pair_pack = swap(jnp.concatenate(near, axis=0), pair)
        own_field, pair_field, rim_field = (
            value.reshape(2, rows, cols) for value in (field, pair_field, rim_field)
        )
        work = 36 * 2 * SUBLANES * cols
        edges = pl.pallas_call(
            functools.partial(inner_kernel, **fixed),
            out_shape=jax.ShapeDtypeStruct(
                (depth - 1, chunks, 2, SUBLANES, LANES), jnp.float32
            ),
            in_specs=[whole] * (3 + sections),
            out_specs=whole,
            scratch_shapes=buffers,
            compiler_params=params,
            cost_estimate=pl.CostEstimate(
                flops=10 * work, bytes_accessed=16 * work, transcendentals=0
            ),
            name="inner_rows",
        )(own_field, pair_field, *own, pair_pack)
        field = pl.pallas_call(
            functools.partial(outer_kernel, tiles=tiles, **fixed),
            out_shape=jax.ShapeDtypeStruct((2, rows, cols), jnp.float32),
            in_specs=[whole] * (4 + sections),
            out_specs=pl.BlockSpec(memory_space=pl.ANY),
            scratch_shapes=[
                pltpu.VMEM((depth, chunks, 2, high, LANES), jnp.float32),
                pltpu.VMEM((sections, chunks, high, LANES), jnp.float32),
                pltpu.VMEM((STAGES, high, LANES), jnp.float32),
                pltpu.VMEM((2, rows, cols), jnp.float32),
                pltpu.SemaphoreType.DMA((OUT_PARTS,)),
            ],
            compiler_params=params,
            name="outer_rows",
        )(own_field, rim_field, *own, rim_pack, edges)[None]
    return field


def solution(mesh):
    placed = (P("sec", None, "tile", None), P("sec", "tile", None))
    return jax.shard_map(
        per_device,
        mesh=mesh,
        in_specs=placed,
        out_specs=P("sec", None, "tile", None),
        check_vma=False,
    )
```

```python
import functools

import jax
import jax.numpy as jnp
from jax import lax
from jax.experimental import pallas as pl
from jax.experimental.pallas import tpu as pltpu
from jax.sharding import PartitionSpec as P

AXES = ("sec", "tile")
LANES = 128
SUBLANES = 8
STAGES = 4
OUT_PARTS = 4

diffract_coef = 0.5
step_length = 0.65


def sec_swap(sec, tiles, k):
    return [(s * tiles + t, (s ^ k) * tiles + t) for s in range(sec) for t in range(tiles)]


def far_bits(k):
    return k ^ (k >> 1)


def pair_swap(sec, tiles):
    return [(s * tiles + t, s * tiles + (t ^ 1)) for s in range(sec) for t in range(tiles)]


def rim_swap(sec, tiles):
    out = []
    for s in range(sec):
        for t in range(tiles):
            if 0 < t < tiles - 1:
                out.append((s * tiles + t, s * tiles + ((t + 1) ^ 1) - 1))
            else:
                out.append((s * tiles + t, (s ^ 1) * tiles + t))
    return out


def stage_scale(stage):
    return diffract_coef * step_length / (STAGES - stage)


def run_stage(source, begin, med, start, blocks, chunks, scale_of, store):
    lane = lax.broadcasted_iota(jnp.int32, (SUBLANES, LANES), 1)
    low_lane, high_lane = lane == 0, lane == LANES - 1
    for j in range(chunks):
        for block in range(blocks):
            at = start + SUBLANES * block
            here = pl.ds(at, SUBLANES)
            m = med[j, here, :]
            g = scale_of(here)
            drive = []
            for part in range(2):
                w = source[j, part, here, :]
                rows_sum = (
                    source[j, part, pl.ds(at - 1, SUBLANES), :]
                    + source[j, part, pl.ds(at + 1, SUBLANES), :]
                )
                before = source[j - 1, part, here, :] if j > 0 else jnp.zeros_like(w)
                after = source[j + 1, part, here, :] if j + 1 < chunks else jnp.zeros_like(w)
                left = pltpu.roll(jnp.where(high_lane, before, w), 1, 1)
                right = pltpu.roll(jnp.where(low_lane, after, w), LANES - 1, 1)
                drive.append(g * (rows_sum + (left + right) + m * w))
            store(j, block, 0, here, begin[j, 0, here, :] - drive[1])
            store(j, block, 1, here, begin[j, 1, here, :] + drive[0])


def row_groups(rows):
    return range(0, rows, SUBLANES)


def columns(j):
    return pl.ds(j * LANES, LANES)


def to_medium_term(value):
    return value * (1.0 / diffract_coef) - 4.0


def by_side(odd, body):
    pl.when(odd == 1)(functools.partial(body, True))
    pl.when(odd == 0)(functools.partial(body, False))


def inner_kernel(*refs, sections, first, rows, cols, steps):
    own_b, pair_b = refs[:2]
    own_m = refs[2 : 2 + sections]
    pair_m = refs[2 + sections : 2 + 2 * sections]
    edge_ref = refs[2 + 2 * sections]
    field_a, field_b, work_a, work_b, med = refs[3 + 2 * sections :]
    sec, odd = lax.axis_index("sec"), lax.axis_index("tile") % 2
    chunks = cols // LANES
    depth = STAGES * steps
    mid = SUBLANES + rows

    def run(is_odd):
        low = SUBLANES if is_odd else mid
        pair_at = SUBLANES if is_odd else mid + rows
        for j in range(chunks):
            col = columns(j)
            for t in row_groups(rows):
                src = pl.ds(t, SUBLANES)
                for part in range(2):
                    field_a[j, part, pl.ds(mid + t, SUBLANES), :] = own_b[part, src, col]
                    field_a[j, part, pl.ds(pair_at + t, SUBLANES), :] = pair_b[part, src, col]
                for k in range(sections):
                    slot = sec ^ far_bits(k)
                    med[slot, j, pl.ds(mid + t, SUBLANES), :] = to_medium_term(
                        own_m[k][0, src, col]
                    )
                    med[slot, j, pl.ds(pair_at + t, SUBLANES), :] = to_medium_term(
                        pair_m[k][0, src, col]
                    )
        begin, end = field_a, field_b
        level = 0
        for step in range(steps):
            source = begin
            for stage in range(STAGES):
                level += 1
                if level == depth:
                    break
                target = (work_a, work_b, work_a, end)[stage]

                def store(j, block, part, here, value, target=target):
                    target[j, part, here, :] = value

                run_stage(
                    source, begin, med.at[first + step], low + level,
                    -(-(2 * (rows - level)) // SUBLANES), chunks,
                    lambda here, stage=stage: stage_scale(stage), store,
                )
                edge_at = mid + rows - SUBLANES - level if is_odd else mid + level
                for j in range(chunks):
                    for part in range(2):
                        edge_ref[level - 1, j, part, :, :] = target[
                            j, part, pl.ds(edge_at, SUBLANES), :
                        ]
                source = target
            begin, end = end, begin

    by_side(odd, run)


def outer_kernel(*refs, tiles, sections, first, rows, cols, steps):
    own_b, rim_b = refs[:2]
    own_m = refs[2 : 2 + sections]
    rim_m, edge_ref, out_ref, levels, med, coef, result, sems = refs[2 + sections :]
    sec, tile = lax.axis_index("sec"), lax.axis_index("tile")
    odd = tile % 2
    chunks = cols // LANES
    depth = STAGES * steps
    mid = SUBLANES + rows
    is_edge = (tile == 0) | (tile == tiles - 1)
    parts = sems.shape[0]
    per_part = chunks // parts

    def run(is_odd):
        rim_at = mid + rows if is_odd else SUBLANES
        row = lax.broadcasted_iota(jnp.int32, coef.shape[1:], 0)
        outside = is_edge & (row >= rim_at) & (row < rim_at + rows)
        for stage in range(STAGES):
            coef[stage] = jnp.where(outside, 0.0, stage_scale(stage))
        for j in range(chunks):
            col = columns(j)
            for t in row_groups(rows):
                src = pl.ds(t, SUBLANES)
                for part in range(2):
                    levels[0, j, part, pl.ds(rim_at + t, SUBLANES), :] = jnp.where(
                        is_edge, 0.0, rim_b[part, src, col]
                    )
            near = rows - SUBLANES if is_odd else 0
            for part in range(2):
                levels[0, j, part, pl.ds(mid + near, SUBLANES), :] = own_b[
                    part, pl.ds(near, SUBLANES), col
                ]
            for k in range(sections):
                for t in row_groups(rows):
                    med[sec ^ far_bits(k), j, pl.ds(mid + t, SUBLANES), :] = to_medium_term(
                        own_m[k][0, pl.ds(t, SUBLANES), col]
                    )
            at = 0
            for step, count in enumerate(rim_rows(rows, steps)):
                over = -count % SUBLANES
                there = mid + rows if is_odd else mid - count - over
                for t in row_groups(count):
                    here = at + t - (0 if is_odd else over)
                    if is_odd and here + SUBLANES > rim_m.shape[1]:
                        size = rim_m.shape[1] - here
                    else:
                        size = SUBLANES
                    med[first + step, j, pl.ds(there + t, size), :] = to_medium_term(
                        rim_m[j, pl.ds(here, size), :]
                    )
                at += count
            for level in range(1, depth):
                edge_at = mid + rows - SUBLANES - level if is_odd else mid + level
                for part in range(2):
                    levels[level, j, part, pl.ds(edge_at, SUBLANES), :] = edge_ref[
                        level - 1, j, part, :, :
                    ]

        copies = [
            pltpu.make_async_copy(
                result.at[:, :, pl.ds(p * per_part * LANES, per_part * LANES)],
                out_ref.at[:, :, pl.ds(p * per_part * LANES, per_part * LANES)],
                sems.at[p],
            )
            for p in range(parts)
        ]
        level = 0
        for step in range(steps):
            begin = levels.at[level]
            for stage in range(STAGES):
                level += 1

                def store(j, block, part, here, value, level=level):
                    if level < depth:
                        levels[level, j, part, here, :] = value
                        return
                    result[part, pl.ds(SUBLANES * block, SUBLANES), columns(j)] = value
                    if part == 1 and block + 1 == rows // SUBLANES and (j + 1) % per_part == 0:
                        copies[j // per_part].start()

                run_stage(
                    levels.at[level - 1], begin, med.at[first + step],
                    mid + depth - level if is_odd else mid + level - depth,
                    rows // SUBLANES, chunks,
                    lambda here, stage=stage: coef[stage, here, :], store,
                )
        for copy in copies:
            copy.wait()

    by_side(odd, run)


def rim_rows(rows, steps):
    return [STAGES * (steps - step) for step in range(steps)]


def pack_kernel(*refs, sections, first, rows, cols, steps):
    own_m, rim_out = refs[:sections], refs[sections]
    sec, odd = lax.axis_index("sec"), lax.axis_index("tile") % 2
    chunks = cols // LANES

    def pack(k, at, lo, hi):
        def body():
            for t in row_groups(rows):
                cut_lo, cut_hi = max(lo, t), min(hi, t + SUBLANES)
                if cut_lo < cut_hi:
                    for j in range(chunks):
                        rim_out[j, pl.ds(at + cut_lo - lo, cut_hi - cut_lo), :] = own_m[k][
                            0, pl.ds(cut_lo, cut_hi - cut_lo), columns(j)
                        ]

        return body

    at = 0
    for step, count in enumerate(rim_rows(rows, steps)):
        for k in range(sections):
            mine = (sec ^ far_bits(k)) == first + step
            pl.when(mine & (odd == 1))(pack(k, at, rows - count, rows))
            pl.when(mine & (odd == 0))(pack(k, at, 0, count))
        at += count


def load_kernel(field_ref, medium_ref, field_out, medium_out, field_sem, medium_sem):
    copies = (
        pltpu.make_async_copy(medium_ref, medium_out, medium_sem),
        pltpu.make_async_copy(field_ref, field_out, field_sem),
    )
    for copy in copies:
        copy.start()
    for copy in copies:
        copy.wait()


def per_device(beams, medium):
    sections, tiles = lax.axis_size("sec"), lax.axis_size("tile")
    _, rows, cols = medium.shape
    swap = lambda value, pairs: lax.ppermute(value, AXES, pairs)
    pair, rim = pair_swap(sections, tiles), rim_swap(sections, tiles)

    far = [swap(medium, sec_swap(sections, tiles, far_bits(k))) for k in range(1, sections)]
    chunks = cols // LANES
    high = 2 * SUBLANES + 3 * rows
    whole = pl.BlockSpec(memory_space=pltpu.VMEM)
    buffers = [pltpu.VMEM((chunks, 2, high, LANES), jnp.float32)] * 4 + [
        pltpu.VMEM((sections, chunks, high, LANES), jnp.float32)
    ]
    params = pltpu.CompilerParams(vmem_limit_bytes=40 * 2**20)
    field, medium = pl.pallas_call(
        load_kernel,
        out_shape=(
            pltpu.VMEM(beams.shape, beams.dtype),
            pltpu.VMEM(medium.shape, medium.dtype),
        ),
        in_specs=[pl.BlockSpec(memory_space=pl.ANY)] * 2,
        out_specs=(whole, whole),
        scratch_shapes=[pltpu.SemaphoreType.DMA(())] * 2,
        cost_estimate=pl.CostEstimate(flops=0, bytes_accessed=2**21, transcendentals=0),
        name="load_arguments",
    )(beams, medium)
    own = [medium] + far
    group = rows // STAGES
    for first in range(0, sections, group):
        steps = min(group, sections - first)
        depth = STAGES * steps
        pair_field = swap(field if first > 0 else beams, pair)
        rim_parts = [swap(field[:, part], rim) for part in range(2)]
        *own, field = lax.optimization_barrier((*own, field))
        fixed = dict(sections=sections, first=first, rows=rows, cols=cols, steps=steps)
        rim_pack = pl.pallas_call(
            functools.partial(pack_kernel, **fixed),
            out_shape=jax.ShapeDtypeStruct(
                (chunks, sum(rim_rows(rows, steps)), LANES), jnp.float32
            ),
            in_specs=[whole] * sections,
            out_specs=whole,
            compiler_params=params,
            name="pack_rows",
        )(*own)
        *near, re, im, _ = lax.optimization_barrier((*own, *rim_parts, rim_pack))
        rim_field = jnp.stack([re, im], axis=1)
        rim_pack = swap(rim_pack, rim)
        pair_m = [swap(piece, pair) for piece in near]
        own_field, pair_field, rim_field = (
            value.reshape(2, rows, cols) for value in (field, pair_field, rim_field)
        )
        work = 36 * 2 * SUBLANES * cols
        edges = pl.pallas_call(
            functools.partial(inner_kernel, **fixed),
            out_shape=jax.ShapeDtypeStruct(
                (depth - 1, chunks, 2, SUBLANES, LANES), jnp.float32
            ),
            in_specs=[whole] * (2 + 2 * sections),
            out_specs=whole,
            scratch_shapes=buffers,
            compiler_params=params,
            cost_estimate=pl.CostEstimate(
                flops=10 * work, bytes_accessed=16 * work, transcendentals=0
            ),
            name="inner_rows",
        )(own_field, pair_field, *own, *pair_m)
        field = pl.pallas_call(
            functools.partial(outer_kernel, tiles=tiles, **fixed),
            out_shape=jax.ShapeDtypeStruct((2, rows, cols), jnp.float32),
            in_specs=[whole] * (4 + sections),
            out_specs=pl.BlockSpec(memory_space=pl.ANY),
            scratch_shapes=[
                pltpu.VMEM((depth, chunks, 2, high, LANES), jnp.float32),
                pltpu.VMEM((sections, chunks, high, LANES), jnp.float32),
                pltpu.VMEM((STAGES, high, LANES), jnp.float32),
                pltpu.VMEM((2, rows, cols), jnp.float32),
                pltpu.SemaphoreType.DMA((OUT_PARTS,)),
            ],
            compiler_params=params,
            name="outer_rows",
        )(own_field, rim_field, *own, rim_pack, edges)[None]
    return field


def solution(mesh):
    placed = (P("sec", None, "tile", None), P("sec", "tile", None))
    return jax.shard_map(
        per_device,
        mesh=mesh,
        in_specs=placed,
        out_specs=P("sec", None, "tile", None),
        check_vma=False,
    )
```
